32 devices in a mesh: groups: 2 (over y), freq: 8 (over z, core), mat: 2 (over x).
Axes of the slice: x: 2, y: 2, z: 4, core: 2. Of those that a mesh axis runs over, the one named last changes fastest.
Arguments:
- traces: bfloat16 [32, 2048, 512], P(('groups', 'freq'), 'mat'), parts along dimension 0, may hold values from -6 to 6
- point_index: int32 [32, 2, 1024], P(('groups', 'freq'), 'mat'), parts along dimension 0, may hold values from 0 to 1023, each once within a row
- spectral_slot_number: int32 [16], P('groups'), parts along dimension 0, may hold values from 1 to 255
Outputs:
- multiples: float32 [32, 8, 2, 16], P(('groups', 'mat'), 'freq'), parts along dimension 0
The draws below stay inside these ranges and needn't reach their ends.
There are 2 independent parts, one for each index of `groups`. The reference program is written for one: setup_inputs(seed, part) draws one part's arguments, and reference() takes and returns one part's arrays. A program takes and returns all parts, laid end to end along the dimension named above; each array names one. Nothing has to cross between parts.
All inputs are finite; a program needn't handle non-finite values.
Results may differ from the reference program's by a relative error of at most 0.0059.
Values may be sent and summed in bfloat16 or wider, within the bound.
A program may use at most 64 MiB of HBM per device.

```python
import math
import jax
import jax.numpy as jnp
from jax import lax

PATCH_POINTS = 2048
NT = 512
SHOTS = 16
FREQS = 8
PB = 1024
NBLK = 2


def place_ends(drawn, key, low, top_value):
    place = [jax.random.randint(jax.random.fold_in(key, axis), (), 0, length) for axis, length in enumerate(drawn.shape)]
    longest = drawn.shape.index(max(drawn.shape))
    beside = place[:longest] + [(place[longest] + 1) % drawn.shape[longest]] + place[longest + 1:]
    return drawn.at[tuple(place)].set(low).at[tuple(beside)].set(top_value)


def with_spikes(array, own_key, source, target, shards_of, factor):
    def block_of(axis_at):
        return (jnp.arange(array.shape[axis_at]) // (array.shape[axis_at] // shards_of)).reshape((-1,) + (1,) * (array.ndim - 1 - axis_at))

    first = jax.random.permutation(own_key, shards_of)[block_of(target)]
    other_side = (block_of(target) + shards_of // 2) % shards_of
    return jnp.where((block_of(source) == first) | (block_of(source) == other_side), factor * array, array)


def shard_levels(key, dims, shards, low, high):
    factor_of, own = 1.0, jax.random.fold_in(key, 6)
    for position, parts in shards:
        steps = jnp.exp(jax.random.uniform(jax.random.fold_in(own, position), (parts,), jnp.float32, low / len(shards), high / len(shards)))
        factor_of = factor_of * jnp.repeat(steps, dims[position] // parts).reshape([-1 if axis == position else 1 for axis in range(len(dims))])
    return factor_of


def heavy_noise(rng, dims, width, most, pieces, heavy, held_as=jnp.bfloat16):
    values = width * jax.random.normal(rng, dims, jnp.float32)
    if pieces:
        values = values * shard_levels(rng, dims, pieces, -0.22, 0.18)
    return jnp.clip(with_spikes(values, jax.random.fold_in(rng, 3), *heavy), -most, most).astype(held_as)


def setup_inputs(seed: int = 0, part: int = 0) -> dict:
    arg_keys = jax.random.split(jax.random.key(seed), 4)
    part_keys = jax.random.split(jax.random.fold_in(arg_keys[3], part), 4)
    return {
        "traces": heavy_noise(part_keys[0], (SHOTS, PATCH_POINTS, NT), 1.0, 6.0, ((0, 8), (1, 2)), (1, 0, 8, 2.0)),
        "point_index": jax.vmap(lambda own: jax.random.permutation(own, PB))(jax.random.split(part_keys[1], SHOTS * NBLK)).reshape((SHOTS, NBLK, PB)).astype(jnp.int32),
        "spectral_slot_number": place_ends(jax.random.randint(part_keys[2], (FREQS,), 1, NT // 2), jax.random.fold_in(part_keys[2], 1), 1, (NT // 2) - 1).astype(jnp.int32),
    }


def fourier_table(spectral_slot_number, record_duration):
    clock_moments = jnp.arange(record_duration, dtype=jnp.int32)
    angular_steps_list = spectral_slot_number.astype(jnp.int32)[:, None] * clock_moments[None, :] % record_duration
    phases = 2.0 * math.pi / record_duration * angular_steps_list.astype(jnp.float32)
    edge_damping_coefficients = 0.5 - 0.5 * jnp.cos(2.0 * math.pi / record_duration * (clock_moments.astype(jnp.float32) + 0.5))
    weighting = edge_damping_coefficients / math.sqrt(record_duration)
    stacked = jnp.stack([jnp.cos(phases) * weighting, -jnp.sin(phases) * weighting], axis=1)
    return stacked.reshape(2 * spectral_slot_number.shape[0], record_duration).astype(jnp.bfloat16)

def reference(traces, point_index, spectral_slot_number):
    fourier = fourier_table(spectral_slot_number, NT)
    raw_spectra = jnp.dot(traces, fourier.T, preferred_element_type=jnp.float32)
    offsets = (jnp.arange(NBLK, dtype=jnp.int32) * PB)[None, :, None]
    columns = (point_index.astype(jnp.int32) + offsets).reshape(SHOTS, PATCH_POINTS)
    spectra = jnp.take_along_axis(raw_spectra, columns[:, :, None], axis=1).astype(jnp.bfloat16)
    spectra = spectra.reshape(SHOTS, PATCH_POINTS, FREQS, 2)
    factor = 4.0 / math.sqrt(PATCH_POINTS)

    def per_frequency(which):
        sliced = lax.dynamic_index_in_dim(spectra, which, 2, keepdims=False)
        real_part = sliced[:, :, 0].astype(jnp.float32)
        imag_part = sliced[:, :, 1].astype(jnp.float32)
        output_real = jnp.dot(real_part, real_part.T) - jnp.dot(imag_part, imag_part.T)
        imag_out = jnp.dot(real_part, imag_part.T) + jnp.dot(imag_part, real_part.T)
        return jnp.stack([output_real, imag_out], axis=0) * factor
    result = lax.map(per_frequency, jnp.arange(FREQS, dtype=jnp.int32))
    return jnp.transpose(result, (2, 0, 1, 3))
```

```python
import functools
import math

import jax
import jax.numpy as jnp
from jax import lax
from jax.experimental import pallas as pl
from jax.experimental.pallas import tpu as pltpu
from jax.sharding import PartitionSpec as P

MESH = pl.DeviceIdType.MESH
LANES = 128
SUB = 8


def sine(x):
    y = x * x
    total = jnp.full_like(y, -1.0 / math.factorial(11))
    for order in (9, 7, 5, 3, 1):
        total = total * y + (-1.0) ** (order // 2) / math.factorial(order)
    return total * x


def cosine_of(turns, period):
    return sine((jnp.abs(turns - 0.5 * period) - 0.25 * period) * (2.0 * math.pi / period))


def kernel(nf, nm, factor, traces_hbm, index_hbm, slots_hbm, out_ref,
           slots, index, traces, table, send, recv, wide, part, land,
           slot_sem, index_sem, trace_sem, send_sem, recv_sem, part_send_sem, part_recv_sem):
    shots, points, moments = traces.shape
    chunks = points // LANES
    halves = trace_sem.shape[1]
    span = points // halves
    me, column = lax.axis_index("freq"), lax.axis_index("mat")

    slot_copy = pltpu.make_async_copy(slots_hbm, slots, slot_sem)
    slot_copy.start()
    trace_copies = []
    for s in range(shots):
        trace_copies.append([])
        for h in range(halves):
            rows = pl.ds(h * span, span)
            copy = pltpu.make_async_copy(traces_hbm.at[s, rows], traces.at[s, rows], trace_sem.at[s, h])
            copy.start()
            trace_copies[s].append(copy)
        if s == 0:
            index_copy = pltpu.make_async_copy(index_hbm, index, index_sem)
            index_copy.start()

    barrier = pltpu.get_barrier_semaphore()
    for k in range(1, nf):
        pl.semaphore_signal(barrier, inc=1, device_id={"freq": lax.rem(me + k, nf)}, device_id_type=MESH)
    for k in range(1, nm):
        pl.semaphore_signal(barrier, inc=1, device_id={"mat": lax.rem(column + k, nm)}, device_id_type=MESH)

    moment = lax.broadcasted_iota(jnp.int32, (SUB, moments), 1)
    taper = 0.5 - 0.5 * cosine_of(moment.astype(jnp.float32) + 0.5, moments)
    weight = taper * (1.0 / math.sqrt(moments))
    row = lax.broadcasted_iota(jnp.int32, (SUB, moments), 0)
    slot_copy.wait()
    for base in range(0, nf, SUB):
        number = jnp.zeros((SUB, moments), jnp.int32)
        for k in range(base, min(base + SUB, nf)):
            number = jnp.where(row == k - base, slots[lax.rem(me + k, nf)], number)
        steps = (number * moment) & (moments - 1)
        quarter = (steps + moments // 4) & (moments - 1)
        pair = [cosine_of(m.astype(jnp.float32), moments) * weight for m in (steps, quarter)]
        for k in range(base, min(base + SUB, nf)):
            both = [jnp.broadcast_to(p[k - base:k - base + 1], (SUB, moments)) for p in pair]
            table[2 * SUB * k:2 * SUB * (k + 1), :] = jnp.concatenate(both, 0).astype(jnp.bfloat16)

    part[...] = jnp.zeros_like(part)
    index_copy.wait()
    copies = {}
    for s in range(shots):
        raw = []
        for h in range(halves):
            trace_copies[s][h].wait()
            raw.append(lax.dot_general(
                table[...], traces[s, h * span:(h + 1) * span, :], (((1,), (1,)), ((), ())),
                preferred_element_type=jnp.float32))
        raw = jnp.concatenate(raw, 1) if halves > 1 else raw[0]
        place = index[s]
        if chunks < SUB:
            place = jnp.concatenate([place] * (SUB // chunks), 0)
        low, high = place & (LANES - 1), place // LANES
        if s == 0:
            pl.semaphore_wait(barrier, nf - 1 + nm - 1)
        for k in list(range(1, nf)) + [0]:
            both = []
            for c in range(2):
                first = (2 * k + c) * SUB
                got = None
                for j in range(chunks):
                    piece = raw[first:first + SUB, j * LANES:(j + 1) * LANES]
                    piece = jnp.take_along_axis(piece, low, axis=1)
                    got = piece if j == 0 else jnp.where(high == j, piece, got)
                both.append(got)
            both = jnp.concatenate(both, 0)
            if k == 0:
                first = pl.multiple_of((me * shots + s) * 2 * SUB, 2 * SUB)
                wide[pl.ds(first, 2 * SUB), :] = both.astype(jnp.bfloat16).astype(jnp.float32)
                continue
            send[s, k] = both.astype(jnp.bfloat16)
            copies[s, k] = pltpu.make_async_remote_copy(
                src_ref=send.at[s, k], dst_ref=recv.at[s, k],
                send_sem=send_sem.at[s, k], recv_sem=recv_sem.at[s, k],
                device_id={"freq": lax.rem(me + k, nf)}, device_id_type=MESH)
            copies[s, k].start()

    for s in range(shots):
        for k in range(1, nf):
            copies[s, k].wait_recv()
            source = lax.rem(me + nf - k, nf)
            first = pl.multiple_of((source * shots + s) * 2 * SUB, 2 * SUB)
            wide[pl.ds(first, 2 * SUB), :] = recv[s, k].astype(jnp.float32)

    count = nf * shots
    real, imag = [
        jnp.concatenate([wide[pl.ds(c * SUB + j, count, stride=2 * SUB), :] for j in range(chunks)], 1)
        for c in range(2)]
    left = jnp.concatenate([real, imag], 1).astype(jnp.bfloat16)
    right = jnp.concatenate(
        [jnp.concatenate([real, -imag], 1), jnp.concatenate([imag, real], 1)], 0).astype(jnp.bfloat16)
    total = lax.dot_general(left, right, (((1,), (1,)), ((), ())), preferred_element_type=jnp.float32)
    total = total * factor
    lines = count // nm
    for m in range(nm):
        part[m, :, :2 * count] = total[m * lines:(m + 1) * lines]
    part_copies = []
    for k in range(1, nm):
        peer = lax.rem(column + k, nm)
        part_copies.append(pltpu.make_async_remote_copy(
            src_ref=part.at[peer], dst_ref=land.at[k - 1],
            send_sem=part_send_sem.at[k - 1], recv_sem=part_recv_sem.at[k - 1],
            device_id={"mat": peer}, device_id_type=MESH))
        part_copies[-1].start()
    result = part[column]
    for k in range(1, nm):
        part_copies[k - 1].wait_recv()
        result = result + land[k - 1]
    out_ref[...] = result

    for copy in list(copies.values()) + part_copies:
        copy.wait_send()


def local(traces, point_index, spectral_slot_number):
    shots, points, moments = traces.shape
    nf, nm = lax.axis_size("freq"), lax.axis_size("mat")
    assert spectral_slot_number.shape[0] == nf and points % LANES == 0
    assert moments & (moments - 1) == 0 and SUB * LANES % points == 0
    count, chunks = nf * shots, points // LANES
    lines = count // nm
    width = -(-2 * count // LANES) * LANES
    halves = 2
    factor = 4.0 / math.sqrt(points * nm)
    index = point_index.reshape(shots, chunks, LANES)
    any_space = pl.BlockSpec(memory_space=pltpu.HBM)
    result = pl.pallas_call(
        functools.partial(kernel, nf, nm, factor),
        out_shape=jax.ShapeDtypeStruct((lines, width), jnp.float32),
        in_specs=[any_space] * 3,
        out_specs=pl.BlockSpec(memory_space=pltpu.VMEM),
        scratch_shapes=[
            pltpu.SMEM(spectral_slot_number.shape, jnp.int32),
            pltpu.VMEM(index.shape, jnp.int32),
            pltpu.VMEM(traces.shape, jnp.bfloat16),
            pltpu.VMEM((2 * SUB * nf, moments), jnp.bfloat16),
            pltpu.VMEM((shots, nf, 2 * SUB, LANES), jnp.bfloat16),
            pltpu.VMEM((shots, nf, 2 * SUB, LANES), jnp.bfloat16),
            pltpu.VMEM((count * 2 * SUB, LANES), jnp.float32),
            pltpu.VMEM((nm, lines, width), jnp.float32),
            pltpu.VMEM((nm - 1, lines, width), jnp.float32),
            pltpu.SemaphoreType.DMA,
            pltpu.SemaphoreType.DMA,
            pltpu.SemaphoreType.DMA((shots, halves)),
            pltpu.SemaphoreType.DMA((shots, nf)),
            pltpu.SemaphoreType.DMA((shots, nf)),
            pltpu.SemaphoreType.DMA((nm - 1,)),
            pltpu.SemaphoreType.DMA((nm - 1,)),
        ],
        compiler_params=pltpu.CompilerParams(
            collective_id=0, has_side_effects=True, vmem_limit_bytes=32 * 1024 * 1024),
    )(traces, index, spectral_slot_number)
    return result[:, :2 * count].reshape(lines, 1, 2, count)


def solution(mesh):
    placed = (P(("groups", "freq"), "mat", None), P(("groups", "freq"), "mat", None), P("groups"))
    return jax.shard_map(
        local,
        mesh=mesh,
        in_specs=placed,
        out_specs=P(("groups", "mat"), "freq", None, None),
        check_vma=False,
    )
```

```python
import functools
import math

import jax
import jax.numpy as jnp
from jax import lax
from jax.experimental import pallas as pl
from jax.experimental.pallas import tpu as pltpu
from jax.sharding import PartitionSpec as P

MESH = pl.DeviceIdType.MESH
LANES = 128
SUB = 8


def sine(x):
    y = x * x
    total = jnp.full_like(y, -1.0 / math.factorial(11))
    for order in (9, 7, 5, 3, 1):
        total = total * y + (-1.0) ** (order // 2) / math.factorial(order)
    return total * x


def cosine_of(turns, period):
    return sine((jnp.abs(turns - 0.5 * period) - 0.25 * period) * (2.0 * math.pi / period))


def kernel(nf, nm, factor, traces_hbm, index_hbm, slots_hbm, out_ref,
           slots, index, traces, table, send, recv, wide, part, land,
           slot_sem, index_sem, trace_sem, send_sem, recv_sem, part_send_sem, part_recv_sem):
    shots, points, moments = traces.shape
    chunks = points // LANES
    halves = trace_sem.shape[1]
    span = points // halves
    me, column = lax.axis_index("freq"), lax.axis_index("mat")

    slot_copy = pltpu.make_async_copy(slots_hbm, slots, slot_sem)
    slot_copy.start()
    trace_copies = []
    for s in range(shots):
        trace_copies.append([])
        for h in range(halves):
            rows = pl.ds(h * span, span)
            copy = pltpu.make_async_copy(traces_hbm.at[s, rows], traces.at[s, rows], trace_sem.at[s, h])
            copy.start()
            trace_copies[s].append(copy)
        if s == 0:
            index_copy = pltpu.make_async_copy(index_hbm, index, index_sem)
            index_copy.start()

    barrier = pltpu.get_barrier_semaphore()
    for k in range(1, nf):
        pl.semaphore_signal(barrier, inc=1, device_id={"freq": lax.rem(me + k, nf)}, device_id_type=MESH)
    for k in range(1, nm):
        pl.semaphore_signal(barrier, inc=1, device_id={"mat": lax.rem(column + k, nm)}, device_id_type=MESH)

    moment = lax.broadcasted_iota(jnp.int32, (SUB, moments), 1)
    taper = 0.5 - 0.5 * cosine_of(moment.astype(jnp.float32) + 0.5, moments)
    weight = taper * (1.0 / math.sqrt(moments))
    row = lax.broadcasted_iota(jnp.int32, (SUB, moments), 0)
    slot_copy.wait()
    for base in range(0, nf, SUB):
        number = jnp.zeros((SUB, moments), jnp.int32)
        for k in range(base, min(base + SUB, nf)):
            number = jnp.where(row == k - base, slots[lax.rem(me + k, nf)], number)
        steps = (number * moment) & (moments - 1)
        quarter = (steps + moments // 4) & (moments - 1)
        pair = [cosine_of(m.astype(jnp.float32), moments) * weight for m in (steps, quarter)]
        for k in range(base, min(base + SUB, nf)):
            both = [jnp.broadcast_to(p[k - base:k - base + 1], (SUB, moments)) for p in pair]
            table[2 * SUB * k:2 * SUB * (k + 1), :] = jnp.concatenate(both, 0).astype(jnp.bfloat16)

    part[...] = jnp.zeros_like(part)
    index_copy.wait()
    copies = {}
    for s in range(shots):
        raw = []
        for h in range(halves):
            trace_copies[s][h].wait()
            raw.append(lax.dot_general(
                table[...], traces[s, h * span:(h + 1) * span, :], (((1,), (1,)), ((), ())),
                preferred_element_type=jnp.float32))
        raw = jnp.concatenate(raw, 1) if halves > 1 else raw[0]
        place = index[s]
        if chunks < SUB:
            place = jnp.concatenate([place] * (SUB // chunks), 0)
        low, high = place & (LANES - 1), place // LANES
        if s == 0:
            pl.semaphore_wait(barrier, nf - 1 + nm - 1)
        for k in list(range(1, nf)) + [0]:
            both = []
            for c in range(2):
                first = (2 * k + c) * SUB
                got = None
                for j in range(chunks):
                    piece = raw[first:first + SUB, j * LANES:(j + 1) * LANES]
                    piece = jnp.take_along_axis(piece, low, axis=1)
                    got = piece if j == 0 else jnp.where(high == j, piece, got)
                both.append(got)
            both = jnp.concatenate(both, 0)
            if k == 0:
                first = pl.multiple_of((me * shots + s) * 2 * SUB, 2 * SUB)
                wide[pl.ds(first, 2 * SUB), :] = both.astype(jnp.bfloat16).astype(jnp.float32)
                continue
            send[s, k] = both.astype(jnp.bfloat16)
            copies[s, k] = pltpu.make_async_remote_copy(
                src_ref=send.at[s, k], dst_ref=recv.at[s, k],
                send_sem=send_sem.at[s, k], recv_sem=recv_sem.at[s, k],
                device_id={"freq": lax.rem(me + k, nf)}, device_id_type=MESH)
            copies[s, k].start()

    for s in range(shots):
        for k in range(1, nf):
            copies[s, k].wait_recv()
            source = lax.rem(me + nf - k, nf)
            first = pl.multiple_of((source * shots + s) * 2 * SUB, 2 * SUB)
            wide[pl.ds(first, 2 * SUB), :] = recv[s, k].astype(jnp.float32)

    count = nf * shots
    real, imag = [
        jnp.concatenate([wide[pl.ds(c * SUB + j, count, stride=2 * SUB), :] for j in range(chunks)], 1)
        for c in range(2)]
    left = jnp.concatenate([real, imag], 1).astype(jnp.bfloat16)
    right = jnp.concatenate(
        [jnp.concatenate([real, -imag], 1), jnp.concatenate([imag, real], 1)], 0).astype(jnp.bfloat16)
    total = lax.dot_general(left, right, (((1,), (1,)), ((), ())), preferred_element_type=jnp.float32)
    total = total * factor
    lines = count // nm
    for m in range(nm):
        part[m, :, :2 * count] = total[m * lines:(m + 1) * lines]
    part_copies = []
    for k in range(1, nm):
        peer = lax.rem(column + k, nm)
        part_copies.append(pltpu.make_async_remote_copy(
            src_ref=part.at[peer], dst_ref=land.at[k - 1],
            send_sem=part_send_sem.at[k - 1], recv_sem=part_recv_sem.at[k - 1],
            device_id={"mat": peer}, device_id_type=MESH))
        part_copies[-1].start()
    result = part[column]
    for k in range(1, nm):
        part_copies[k - 1].wait_recv()
        result = result + land[k - 1]
    out_ref[...] = result

    for copy in list(copies.values()) + part_copies:
        copy.wait_send()


def local(traces, point_index, spectral_slot_number):
    shots, points, moments = traces.shape
    nf, nm = lax.axis_size("freq"), lax.axis_size("mat")
    assert spectral_slot_number.shape[0] == nf and points % LANES == 0
    assert moments & (moments - 1) == 0 and SUB * LANES % points == 0
    count, chunks = nf * shots, points // LANES
    lines = count // nm
    width = -(-2 * count // LANES) * LANES
    halves = 2
    factor = 4.0 / math.sqrt(points * nm)
    index = point_index.reshape(shots, chunks, LANES)
    any_space = pl.BlockSpec(memory_space=pltpu.HBM)
    result = pl.pallas_call(
        functools.partial(kernel, nf, nm, factor),
        out_shape=pltpu.VMEM((lines, width), jnp.float32),
        in_specs=[any_space] * 3,
        out_specs=pl.BlockSpec(memory_space=pltpu.VMEM),
        scratch_shapes=[
            pltpu.SMEM(spectral_slot_number.shape, jnp.int32),
            pltpu.VMEM(index.shape, jnp.int32),
            pltpu.VMEM(traces.shape, jnp.bfloat16),
            pltpu.VMEM((2 * SUB * nf, moments), jnp.bfloat16),
            pltpu.VMEM((shots, nf, 2 * SUB, LANES), jnp.bfloat16),
            pltpu.VMEM((shots, nf, 2 * SUB, LANES), jnp.bfloat16),
            pltpu.VMEM((count * 2 * SUB, LANES), jnp.float32),
            pltpu.VMEM((nm, lines, width), jnp.float32),
            pltpu.VMEM((nm - 1, lines, width), jnp.float32),
            pltpu.SemaphoreType.DMA,
            pltpu.SemaphoreType.DMA,
            pltpu.SemaphoreType.DMA((shots, halves)),
            pltpu.SemaphoreType.DMA((shots, nf)),
            pltpu.SemaphoreType.DMA((shots, nf)),
            pltpu.SemaphoreType.DMA((nm - 1,)),
            pltpu.SemaphoreType.DMA((nm - 1,)),
        ],
        compiler_params=pltpu.CompilerParams(
            collective_id=0, has_side_effects=True, vmem_limit_bytes=60 * 1024 * 1024),
    )(traces, index, spectral_slot_number)
    return result[:, :2 * count].reshape(lines, 1, 2, count)


def solution(mesh):
    placed = (P(("groups", "freq"), "mat", None), P(("groups", "freq"), "mat", None), P("groups"))
    return jax.shard_map(
        local,
        mesh=mesh,
        in_specs=placed,
        out_specs=P(("groups", "mat"), "freq", None, None),
        check_vma=False,
    )
```

```python
import functools
import math

import jax
import jax.numpy as jnp
from jax import lax
from jax.experimental import pallas as pl
from jax.experimental.pallas import tpu as pltpu
from jax.sharding import PartitionSpec as P

MESH = pl.DeviceIdType.MESH
LANES = 128
SUB = 8


def sine(x):
    y = x * x
    total = jnp.full_like(y, -1.0 / math.factorial(11))
    for order in (9, 7, 5, 3, 1):
        total = total * y + (-1.0) ** (order // 2) / math.factorial(order)
    return total * x


def cosine_of(turns, period):
    return sine((jnp.abs(turns - 0.5 * period) - 0.25 * period) * (2.0 * math.pi / period))


def kernel(nf, nm, factor, traces_hbm, index_hbm, slots_hbm, out_ref,
           slots, index, traces, table, send, recv, wide, whole,
           slot_sem, index_sem, trace_sem, send_sem, recv_sem):
    shots, points, moments = traces.shape
    chunks = points // LANES
    halves = trace_sem.shape[1]
    span = points // halves
    me, column = lax.axis_index("freq"), lax.axis_index("mat")
    peers = [(k, j) for k in list(range(1, nf)) + [0] for j in range(nm) if k or j]

    def device(k, j):
        return {"freq": lax.rem(me + k, nf), "mat": lax.rem(column + j, nm)}

    barrier = pltpu.get_barrier_semaphore()
    for k, j in peers:
        pl.semaphore_signal(barrier, inc=1, device_id=device(k, j), device_id_type=MESH)

    slot_copy = pltpu.make_async_copy(slots_hbm, slots, slot_sem)
    slot_copy.start()
    trace_copies = []
    for s in range(shots):
        trace_copies.append([])
        for h in range(halves):
            rows = pl.ds(h * span, span)
            copy = pltpu.make_async_copy(traces_hbm.at[s, rows], traces.at[s, rows], trace_sem.at[s, h])
            copy.start()
            trace_copies[s].append(copy)
        if s == 0:
            index_copy = pltpu.make_async_copy(index_hbm, index, index_sem)
            index_copy.start()

    moment = lax.broadcasted_iota(jnp.int32, (SUB, moments), 1)
    taper = 0.5 - 0.5 * cosine_of(moment.astype(jnp.float32) + 0.5, moments)
    weight = taper * (1.0 / math.sqrt(moments))
    row = lax.broadcasted_iota(jnp.int32, (SUB, moments), 0)
    slot_copy.wait()
    for base in range(0, nf, SUB):
        number = jnp.zeros((SUB, moments), jnp.int32)
        for k in range(base, min(base + SUB, nf)):
            number = jnp.where(row == k - base, slots[lax.rem(me + k, nf)], number)
        steps = (number * moment) & (moments - 1)
        quarter = (steps + moments // 4) & (moments - 1)
        pair = [cosine_of(m.astype(jnp.float32), moments) * weight for m in (steps, quarter)]
        for k in range(base, min(base + SUB, nf)):
            both = [jnp.broadcast_to(p[k - base:k - base + 1], (SUB, moments)) for p in pair]
            table[2 * SUB * k:2 * SUB * (k + 1), :] = jnp.concatenate(both, 0).astype(jnp.bfloat16)

    copies = {}

    def start(s, k):
        for j in range(nm):
            if k or j:
                copies[s, k, j] = pltpu.make_async_remote_copy(
                    src_ref=send.at[s, k], dst_ref=recv.at[j, s, k],
                    send_sem=send_sem.at[j, s, k], recv_sem=recv_sem.at[j, s, k],
                    device_id=device(k, j), device_id_type=MESH)
                copies[s, k, j].start()

    order = list(range(1, nf)) + [0]
    index_copy.wait()
    for s in range(shots):
        raw = []
        for h in range(halves):
            trace_copies[s][h].wait()
            raw.append(lax.dot_general(
                table[...], traces[s, h * span:(h + 1) * span, :], (((1,), (1,)), ((), ())),
                preferred_element_type=jnp.float32))
        raw = jnp.concatenate(raw, 1) if halves > 1 else raw[0]
        place = index[s]
        if chunks < SUB:
            place = jnp.concatenate([place] * (SUB // chunks), 0)
        low, high = place & (LANES - 1), place // LANES
        for k in order:
            both = []
            for c in range(2):
                first = (2 * k + c) * SUB
                got = None
                for j in range(chunks):
                    piece = raw[first:first + SUB, j * LANES:(j + 1) * LANES]
                    piece = jnp.take_along_axis(piece, low, axis=1)
                    got = piece if j == 0 else jnp.where(high == j, piece, got)
                both.append(got)
            send[s, k] = jnp.concatenate(both, 0).astype(jnp.bfloat16)
            if s:
                start(s, k)
        if s == 0:
            pl.semaphore_wait(barrier, len(peers))
            for k in order:
                start(s, k)

    count = nf * shots
    total = None
    for j in range(nm):
        for s in range(shots):
            for k in range(nf):
                if k or j:
                    copies[s, k, j].wait_recv()
                    block = recv[j, s, k]
                else:
                    block = send[s, k]
                source = lax.rem(me + nf - k, nf)
                first = pl.multiple_of((source * shots + s) * 2 * SUB, 2 * SUB)
                wide[j, pl.ds(first, 2 * SUB), :] = block.astype(jnp.float32)
        real, imag = [
            jnp.concatenate([wide[j, pl.ds(c * SUB + i, count, stride=2 * SUB), :] for i in range(chunks)], 1)
            for c in range(2)]
        left = jnp.concatenate([real, imag], 1).astype(jnp.bfloat16)
        right = jnp.concatenate(
            [jnp.concatenate([real, -imag], 1), jnp.concatenate([imag, real], 1)], 0).astype(jnp.bfloat16)
        term = lax.dot_general(left, right, (((1,), (1,)), ((), ())), preferred_element_type=jnp.float32)
        total = term if j == 0 else total + term
    lines = count // nm
    whole[:, :2 * count] = total * factor
    out_ref[:, :2 * count] = whole[pl.ds(pl.multiple_of(column * lines, lines), lines), :2 * count]

    for copy in copies.values():
        copy.wait_send()


def local(traces, point_index, spectral_slot_number):
    shots, points, moments = traces.shape
    nf, nm = lax.axis_size("freq"), lax.axis_size("mat")
    assert spectral_slot_number.shape[0] == nf and points % LANES == 0
    assert moments & (moments - 1) == 0 and SUB * LANES % points == 0
    count, chunks = nf * shots, points // LANES
    lines = count // nm
    width = -(-2 * count // LANES) * LANES
    halves = 2
    factor = 4.0 / math.sqrt(points * nm)
    index = point_index.reshape(shots, chunks, LANES)
    any_space = pl.BlockSpec(memory_space=pltpu.HBM)
    result = pl.pallas_call(
        functools.partial(kernel, nf, nm, factor),
        out_shape=pltpu.VMEM((lines, width), jnp.float32),
        in_specs=[any_space] * 3,
        out_specs=pl.BlockSpec(memory_space=pltpu.VMEM),
        scratch_shapes=[
            pltpu.SMEM(spectral_slot_number.shape, jnp.int32),
            pltpu.VMEM(index.shape, jnp.int32),
            pltpu.VMEM(traces.shape, jnp.bfloat16),
            pltpu.VMEM((2 * SUB * nf, moments), jnp.bfloat16),
            pltpu.VMEM((shots, nf, 2 * SUB, LANES), jnp.bfloat16),
            pltpu.VMEM((nm, shots, nf, 2 * SUB, LANES), jnp.bfloat16),
            pltpu.VMEM((nm, count * 2 * SUB, LANES), jnp.float32),
            pltpu.VMEM((count, width), jnp.float32),
            pltpu.SemaphoreType.DMA,
            pltpu.SemaphoreType.DMA,
            pltpu.SemaphoreType.DMA((shots, halves)),
            pltpu.SemaphoreType.DMA((nm, shots, nf)),
            pltpu.SemaphoreType.DMA((nm, shots, nf)),
        ],
        compiler_params=pltpu.CompilerParams(
            collective_id=0, has_side_effects=True, vmem_limit_bytes=60 * 1024 * 1024),
    )(traces, index, spectral_slot_number)
    return result[:, :2 * count].reshape(lines, 1, 2, count)


def solution(mesh):
    placed = (P(("groups", "freq"), "mat", None), P(("groups", "freq"), "mat", None), P("groups"))
    return jax.shard_map(
        local,
        mesh=mesh,
        in_specs=placed,
        out_specs=P(("groups", "mat"), "freq", None, None),
        check_vma=False,
    )
```

```python
import functools
import math

import jax
import jax.numpy as jnp
from jax import lax
from jax.experimental import pallas as pl
from jax.experimental.pallas import tpu as pltpu
from jax.sharding import PartitionSpec as P

MESH = pl.DeviceIdType.MESH
LANES = 128
SUB = 8


def sine(x):
    y = x * x
    total = jnp.full_like(y, -1.0 / math.factorial(11))
    for order in (9, 7, 5, 3, 1):
        total = total * y + (-1.0) ** (order // 2) / math.factorial(order)
    return total * x


def cosine_of(turns, period):
    return sine((jnp.abs(turns - 0.5 * period) - 0.25 * period) * (2.0 * math.pi / period))


def kernel(nf, nm, factor, traces_hbm, index_hbm, slots_hbm, out_ref,
           slots, index, traces, table, send, recv, wide, whole,
           slot_sem, index_sem, trace_sem, send_sem, recv_sem):
    shots, points, moments = traces.shape
    chunks = points // LANES
    halves = trace_sem.shape[1]
    span = points // halves
    me, column = lax.axis_index("freq"), lax.axis_index("mat")
    peers = [(k, j) for k in list(range(1, nf)) + [0] for j in range(nm) if k or j]

    def device(k, j):
        return {"freq": lax.rem(me + k, nf), "mat": lax.rem(column + j, nm)}

    slot_copy = pltpu.make_async_copy(slots_hbm, slots, slot_sem)
    slot_copy.start()
    trace_copies = []
    for s in range(shots):
        trace_copies.append([])
        for h in range(halves):
            rows = pl.ds(h * span, span)
            copy = pltpu.make_async_copy(traces_hbm.at[s, rows], traces.at[s, rows], trace_sem.at[s, h])
            copy.start()
            trace_copies[s].append(copy)
        if s == 0:
            index_copy = pltpu.make_async_copy(index_hbm, index, index_sem)
            index_copy.start()

    barrier = pltpu.get_barrier_semaphore()
    for k, j in peers:
        pl.semaphore_signal(barrier, inc=1, device_id=device(k, j), device_id_type=MESH)

    moment = lax.broadcasted_iota(jnp.int32, (SUB, moments), 1)
    taper = 0.5 - 0.5 * cosine_of(moment.astype(jnp.float32) + 0.5, moments)
    weight = taper * (1.0 / math.sqrt(moments))
    row = lax.broadcasted_iota(jnp.int32, (SUB, moments), 0)
    slot_copy.wait()
    for base in range(0, nf, SUB):
        number = jnp.zeros((SUB, moments), jnp.int32)
        for k in range(base, min(base + SUB, nf)):
            number = jnp.where(row == k - base, slots[lax.rem(me + k, nf)], number)
        steps = (number * moment) & (moments - 1)
        quarter = (steps + moments // 4) & (moments - 1)
        pair = [cosine_of(m.astype(jnp.float32), moments) * weight for m in (steps, quarter)]
        for k in range(base, min(base + SUB, nf)):
            both = [jnp.broadcast_to(p[k - base:k - base + 1], (SUB, moments)) for p in pair]
            table[2 * SUB * k:2 * SUB * (k + 1), :] = jnp.concatenate(both, 0).astype(jnp.bfloat16)

    copies = {}

    def start(k):
        for j in reversed(range(nm)):
            if k or j:
                copies[k, j] = pltpu.make_async_remote_copy(
                    src_ref=send.at[k], dst_ref=recv.at[j, k],
                    send_sem=send_sem.at[j, k], recv_sem=recv_sem.at[j, k],
                    device_id=device(k, j), device_id_type=MESH)
                copies[k, j].start()

    order = list(range(1, nf)) + [0]
    index_copy.wait()
    for s in range(shots):
        raw = []
        for h in range(halves):
            trace_copies[s][h].wait()
            raw.append(lax.dot_general(
                table[...], traces[s, h * span:(h + 1) * span, :], (((1,), (1,)), ((), ())),
                preferred_element_type=jnp.float32))
        raw = jnp.concatenate(raw, 1) if halves > 1 else raw[0]
        place = index[s]
        if chunks < SUB:
            place = jnp.concatenate([place] * (SUB // chunks), 0)
        low, high = place & (LANES - 1), place // LANES
        for k in order:
            both = []
            for c in range(2):
                first = (2 * k + c) * SUB
                got = None
                for j in range(chunks):
                    piece = raw[first:first + SUB, j * LANES:(j + 1) * LANES]
                    piece = jnp.take_along_axis(piece, low, axis=1)
                    got = piece if j == 0 else jnp.where(high == j, piece, got)
                both.append(got)
            send[k, s] = jnp.concatenate(both, 0).astype(jnp.bfloat16)
        if s == shots - 1:
            pl.semaphore_wait(barrier, len(peers))
            for k in order:
                start(k)

    count = nf * shots
    total = None
    for j in range(nm):
        for s in range(shots):
            for k in range(nf):
                if k or j:
                    if s == 0:
                        copies[k, j].wait_recv()
                    block = recv[j, k, s]
                else:
                    block = send[k, s]
                source = lax.rem(me + nf - k, nf)
                first = pl.multiple_of((source * shots + s) * 2 * SUB, 2 * SUB)
                wide[j, pl.ds(first, 2 * SUB), :] = block.astype(jnp.float32)
        real, imag = [
            jnp.concatenate([wide[j, pl.ds(c * SUB + i, count, stride=2 * SUB), :] for i in range(chunks)], 1)
            for c in range(2)]
        left = jnp.concatenate([real, imag], 1).astype(jnp.bfloat16)
        right = jnp.concatenate(
            [jnp.concatenate([real, -imag], 1), jnp.concatenate([imag, real], 1)], 0).astype(jnp.bfloat16)
        term = lax.dot_general(left, right, (((1,), (1,)), ((), ())), preferred_element_type=jnp.float32)
        total = term if j == 0 else total + term
    lines = count // nm
    whole[:, :2 * count] = total * factor
    out_ref[:, :2 * count] = whole[pl.ds(pl.multiple_of(column * lines, lines), lines), :2 * count]

    for copy in copies.values():
        copy.wait_send()


def local(traces, point_index, spectral_slot_number):
    shots, points, moments = traces.shape
    nf, nm = lax.axis_size("freq"), lax.axis_size("mat")
    assert spectral_slot_number.shape[0] == nf and points % LANES == 0
    assert moments & (moments - 1) == 0 and SUB * LANES % points == 0
    count, chunks = nf * shots, points // LANES
    lines = count // nm
    width = -(-2 * count // LANES) * LANES
    halves = 1
    factor = 4.0 / math.sqrt(points * nm)
    index = point_index.reshape(shots, chunks, LANES)
    any_space = pl.BlockSpec(memory_space=pltpu.HBM)
    result = pl.pallas_call(
        functools.partial(kernel, nf, nm, factor),
        out_shape=pltpu.VMEM((lines, width), jnp.float32),
        in_specs=[any_space] * 3,
        out_specs=pl.BlockSpec(memory_space=pltpu.VMEM),
        scratch_shapes=[
            pltpu.SMEM(spectral_slot_number.shape, jnp.int32),
            pltpu.VMEM(index.shape, jnp.int32),
            pltpu.VMEM(traces.shape, jnp.bfloat16),
            pltpu.VMEM((2 * SUB * nf, moments), jnp.bfloat16),
            pltpu.VMEM((nf, shots, 2 * SUB, LANES), jnp.bfloat16),
            pltpu.VMEM((nm, nf, shots, 2 * SUB, LANES), jnp.bfloat16),
            pltpu.VMEM((nm, count * 2 * SUB, LANES), jnp.float32),
            pltpu.VMEM((count, width), jnp.float32),
            pltpu.SemaphoreType.DMA,
            pltpu.SemaphoreType.DMA,
            pltpu.SemaphoreType.DMA((shots, halves)),
            pltpu.SemaphoreType.DMA((nm, nf)),
            pltpu.SemaphoreType.DMA((nm, nf)),
        ],
        compiler_params=pltpu.CompilerParams(
            collective_id=0, has_side_effects=True, vmem_limit_bytes=60 * 1024 * 1024),
    )(traces, index, spectral_slot_number)
    return result[:, :2 * count].reshape(lines, 1, 2, count)


def solution(mesh):
    placed = (P(("groups", "freq"), "mat", None), P(("groups", "freq"), "mat", None), P("groups"))
    return jax.shard_map(
        local,
        mesh=mesh,
        in_specs=placed,
        out_specs=P(("groups", "mat"), "freq", None, None),
        check_vma=False,
    )
```
